256 devices in a mesh: head: 4 (over x_hi, core), loop: 64 (over x_lo, y, z).
Axes of the slice: x: 4 (x_hi: 2, x_lo: 2; x = x_hi * 2 + x_lo), y: 4, z: 8, core: 2. Of those that a mesh axis runs over, the one named last changes fastest.
Arguments:
- prompt_query_rows: bfloat16 [8192, 4096], P('loop', 'head'), as said below
- prompt_key_rows: bfloat16 [8192, 512], P('loop', 'head'), as said below
- prompt_value_rows: bfloat16 [8192, 512], P('loop', 'head'), may hold values from -6 to 6
- tail_query_rows: bfloat16 [64, 64, 4096], P('loop', None, 'head'), as said below
- tail_key_rows: bfloat16 [64, 64, 512], P('loop', None, 'head'), as said below
- tail_value_rows: bfloat16 [64, 64, 512], P('loop', None, 'head'), may hold values from -6 to 6
- tail_len: int32 [64], P('loop'), may hold values from 1 to 64, as said below
- stretch_order: int32 [128], replicated, may hold values from 0 to 127, each once
- out_weight: bfloat16 [4096, 5120], P('head'), may hold values from -0.09375 to 0.09375
Outputs:
- prompt_out: bfloat16 [8192, 5120], P('loop', 'head')
- tail_out: bfloat16 [64, 64, 5120], P('loop', None, 'head')
The draws below stay inside these ranges and needn't reach their ends.
Inputs may be any that keep to these rules, and one draw needn't show every extreme that they name: `prompt_query_rows`: prompt queries. `prompt_key_rows`: prompt keys. `tail_query_rows`: tail queries. `tail_key_rows`: tail keys. `tail_len`: at least one tail has all 64 slots valid. A permutation: stored block j holds the prompt positions stretch_order[j] * 64 to stretch_order[j] * 64 + 63 in order.
All inputs are finite; a program needn't handle non-finite values.
Results may differ from the reference program's by a relative error of at most 0.015.
Values may be sent and summed in bfloat16 or wider, within the bound.
A program may use at most 64 MiB of HBM per device.

```python
import math
import jax
import jax.numpy as jnp
from jax import lax

D = 5120
QUERY_HEADS = 32
KEY_VALUE_HEADS = 4
HEAD_SIZE = 128
CH = 64
TAIL_SLOTS = 64
SAMPLE_TAILS = 64
NCH = 128
PROMPT_TOKENS = 8192


def prompt_base(key):
    return jax.random.normal(jax.random.fold_in(key, 101), (PROMPT_TOKENS, KEY_VALUE_HEADS * HEAD_SIZE), jnp.float32)


def tail_base(key):
    return jax.random.normal(jax.random.fold_in(key, 202), (SAMPLE_TAILS, TAIL_SLOTS, KEY_VALUE_HEADS * HEAD_SIZE), jnp.float32)


def spread_heads(start_offset):
    leading_rows = start_offset.shape[:-1]
    split_point = start_offset.reshape(leading_rows + (KEY_VALUE_HEADS, 1, HEAD_SIZE))
    return jnp.repeat(split_point, QUERY_HEADS // KEY_VALUE_HEADS, axis=-2).reshape(leading_rows + (QUERY_HEADS * HEAD_SIZE,))


def draw_prompt_key_rows(key, part):
    start_offset = prompt_base(key)
    return start_offset.astype(jnp.bfloat16)


def draw_prompt_query_rows(key, part):
    key = jax.random.fold_in(key, 5)
    fresh = 2.5 * jax.random.normal(key, (PROMPT_TOKENS, QUERY_HEADS * HEAD_SIZE), jnp.float32)
    return fresh.astype(jnp.bfloat16)


def draw_tail_key_rows(key, part):
    start_offset = tail_base(key)
    return start_offset.astype(jnp.bfloat16)


def draw_tail_query_rows(key, part):
    start_offset = tail_base(key)
    key = jax.random.fold_in(key, 13)
    fresh = 2.5 * jax.random.normal(key, (SAMPLE_TAILS, TAIL_SLOTS, QUERY_HEADS * HEAD_SIZE), jnp.float32)
    aligned = spread_heads(start_offset)
    mixed = fresh + aligned
    return mixed.astype(jnp.bfloat16)


def draw_tail_len(key, part):
    key = jax.random.fold_in(key, 11)
    lengths = jax.random.randint(key, (SAMPLE_TAILS,), 1, TAIL_SLOTS + 1)
    spot = jax.random.randint(jax.random.fold_in(key, 1), (), 0, SAMPLE_TAILS)
    return jnp.where(jnp.arange(SAMPLE_TAILS) == spot, TAIL_SLOTS, lengths).astype(jnp.int32)


def levels(rng, dims, cuts, smallest, top_value):
    factor_of = 1.0
    for axis_at, shards_of in cuts:
        heights = jax.random.uniform(jax.random.fold_in(jax.random.fold_in(rng, 6), axis_at), (shards_of,), jnp.float32, smallest / len(cuts), top_value / len(cuts))
        factor_of = factor_of * jnp.repeat(jnp.exp(heights), dims[axis_at] // shards_of).reshape((-1,) + (1,) * (len(dims) - 1 - axis_at))
    return factor_of


def normal_values(rng, dims, scale, most, pieces=(), held_as=jnp.bfloat16):
    loudness = levels(rng, dims, pieces, -0.22, 0.18) if pieces else 1.0
    array = jax.random.normal(rng, dims, jnp.float32) * scale * loudness
    return jnp.minimum(jnp.maximum(array, -most), most).astype(held_as)


def setup_inputs(seed: int = 0) -> dict:
    splits = jax.random.split(jax.random.key(seed), 10)
    return {
        "prompt_query_rows": draw_prompt_query_rows(jax.random.fold_in(splits[9], 71), 0),
        "prompt_key_rows": draw_prompt_key_rows(jax.random.fold_in(splits[9], 71), 0),
        "prompt_value_rows": normal_values(splits[2], (PROMPT_TOKENS, KEY_VALUE_HEADS * HEAD_SIZE), 1.0, 6.0, ((0, 64), (1, 4))),
        "tail_query_rows": draw_tail_query_rows(jax.random.fold_in(splits[9], 71), 0),
        "tail_key_rows": draw_tail_key_rows(jax.random.fold_in(splits[9], 71), 0),
        "tail_value_rows": normal_values(splits[5], (SAMPLE_TAILS, TAIL_SLOTS, KEY_VALUE_HEADS * HEAD_SIZE), 1.0, 6.0, ((0, 64), (2, 4))),
        "tail_len": draw_tail_len(jax.random.fold_in(splits[9], 71), 0),
        "stretch_order": jax.random.permutation(splits[7], NCH).astype(jnp.int32),
        "out_weight": normal_values(splits[8], (QUERY_HEADS * HEAD_SIZE, D), (QUERY_HEADS * HEAD_SIZE) ** -0.5, 0.09375, ((0, 4),)),
    }


NEGATIVE = -1e+30

def rounded(weights):
    return lax.optimization_barrier(weights.astype(jnp.bfloat16)).astype(jnp.float32)

def reference(prompt_query_rows, prompt_key_rows, prompt_value_rows, tail_query_rows, tail_key_rows, tail_value_rows, tail_len, stretch_order, out_weight):
    query_groups = QUERY_HEADS // KEY_VALUE_HEADS
    scale = 1.0 / math.sqrt(HEAD_SIZE)
    rows = jnp.arange(PROMPT_TOKENS, dtype=jnp.int32)
    positions = stretch_order[rows // CH].astype(jnp.int32) * CH + rows % CH
    query_grouped = prompt_query_rows.reshape(PROMPT_TOKENS, KEY_VALUE_HEADS, query_groups, HEAD_SIZE)
    joined_keys = prompt_key_rows.reshape(PROMPT_TOKENS, KEY_VALUE_HEADS, HEAD_SIZE).astype(jnp.float32)
    joined_values = prompt_value_rows.reshape(PROMPT_TOKENS, KEY_VALUE_HEADS, HEAD_SIZE).astype(jnp.float32)
    block = min(512, PROMPT_TOKENS)

    def single_head(head):
        head_q = lax.dynamic_index_in_dim(query_grouped, head, 1, keepdims=False)
        head_k = lax.dynamic_index_in_dim(joined_keys, head, 1, keepdims=False)
        head_v = lax.dynamic_index_in_dim(joined_values, head, 1, keepdims=False)

        def one_block(index):
            start = (index * block).astype(jnp.int32)
            block_q = lax.dynamic_slice_in_dim(head_q, start, block, 0).astype(jnp.float32)
            block_pos = lax.dynamic_slice_in_dim(positions, start, block, 0)
            scores = jnp.einsum('rgd,nd->rgn', block_q, head_k) * scale
            visible = positions[None, None, :] <= block_pos[:, None, None]
            scores = jnp.where(visible, scores, NEGATIVE)
            top = lax.optimization_barrier(jnp.max(scores, axis=-1, keepdims=True))
            weights = jnp.where(visible, jnp.exp(scores - top), 0.0)
            denom = lax.optimization_barrier(jnp.sum(weights, axis=-1))
            mixed = jnp.einsum('rgn,nd->rgd', rounded(weights), head_v)
            return mixed / denom[..., None]
        out = lax.map(one_block, jnp.arange(PROMPT_TOKENS // block, dtype=jnp.int32))
        return out.reshape(PROMPT_TOKENS, query_groups, HEAD_SIZE)
    prompt_attended = lax.map(single_head, jnp.arange(KEY_VALUE_HEADS, dtype=jnp.int32))
    prompt_heads = jnp.transpose(prompt_attended, (1, 0, 2, 3)).reshape(PROMPT_TOKENS, QUERY_HEADS * HEAD_SIZE)
    steps = jnp.arange(TAIL_SLOTS, dtype=jnp.int32)
    tail_grouped = tail_query_rows.reshape(SAMPLE_TAILS, TAIL_SLOTS, KEY_VALUE_HEADS, query_groups, HEAD_SIZE)
    tail_joined_keys = tail_key_rows.reshape(SAMPLE_TAILS, TAIL_SLOTS, KEY_VALUE_HEADS, HEAD_SIZE)
    tail_joined_values = tail_value_rows.reshape(SAMPLE_TAILS, TAIL_SLOTS, KEY_VALUE_HEADS, HEAD_SIZE)

    def one_sample(index):
        sample_q = lax.dynamic_index_in_dim(tail_grouped, index, 0, keepdims=False).astype(jnp.float32)
        sample_k = lax.dynamic_index_in_dim(tail_joined_keys, index, 0, keepdims=False).astype(jnp.float32)
        sample_v = lax.dynamic_index_in_dim(tail_joined_values, index, 0, keepdims=False).astype(jnp.float32)
        limit = lax.dynamic_index_in_dim(tail_len, index, 0, keepdims=False)
        early = jnp.einsum('tkgd,nkd->tkgn', sample_q, joined_keys) * scale
        late = jnp.einsum('tkgd,nkd->tkgn', sample_q, sample_k) * scale
        visible = (steps[None, :] <= steps[:, None]) & (steps[None, :] < limit)
        late = jnp.where(visible[:, None, None, :], late, NEGATIVE)
        top = jnp.maximum(lax.optimization_barrier(jnp.max(early, axis=-1)), lax.optimization_barrier(jnp.max(late, axis=-1)))[..., None]
        early_w = jnp.exp(early - top)
        late_w = jnp.where(visible[:, None, None, :], jnp.exp(late - top), 0.0)
        denom = lax.optimization_barrier(jnp.sum(early_w, axis=-1)) + lax.optimization_barrier(jnp.sum(late_w, axis=-1))
        mixed = jnp.einsum('tkgn,nkd->tkgd', rounded(early_w), joined_values)
        mixed = mixed + jnp.einsum('tkgn,nkd->tkgd', rounded(late_w), sample_v)
        mixed = mixed / denom[..., None]
        live = steps < limit
        return jnp.where(live[:, None, None, None], mixed, 0.0).reshape(TAIL_SLOTS, QUERY_HEADS * HEAD_SIZE)
    tail_heads = lax.map(one_sample, jnp.arange(SAMPLE_TAILS, dtype=jnp.int32)).reshape(SAMPLE_TAILS * TAIL_SLOTS, QUERY_HEADS * HEAD_SIZE)
    heads_all = jnp.concatenate([prompt_heads, tail_heads], axis=0).astype(jnp.bfloat16)
    projected = jnp.dot(heads_all, out_weight, preferred_element_type=jnp.float32).astype(jnp.bfloat16)
    return (projected[:PROMPT_TOKENS], projected[PROMPT_TOKENS:].reshape(SAMPLE_TAILS, TAIL_SLOTS, D))
```

```python
import functools
import math

import jax
import jax.numpy as jnp
from jax import lax
from jax.experimental import pallas as pl
from jax.experimental.pallas import tpu as pltpu
from jax.sharding import PartitionSpec as P

F32, BF16 = jnp.float32, jnp.bfloat16
MESH = pl.DeviceIdType.MESH
NT = (((1,), (1,)), ((), ()))
HIDDEN = -1e30
RATE = math.log2(math.e) / math.sqrt(128.0)
STEPS = (0, 1, -1, 2, -2, 3, -3, 4)
PLACE = {0: 0, 1: 1, -1: 2, 2: 3, -2: 4, 3: 5, -3: 6, 4: 7, -4: 7}
BATCHES = ((0, 1), (1, 3), (3, 5), (5, 8))
LINES = (0, 1, -1, 2)


def kernel(
    pq, pk, pv, tq, tk, tv, tail_len, order, weight,
    prompt_out, tail_out,
    kv, q, tkv, hot, wv, qs, acc, top, mixed, mine, half_out, half_in, kept, cross_out, cross_in,
    send_sem, recv_sem, local_sem,
):
    head, loop = lax.axis_index("head"), lax.axis_index("loop")
    xh, c = head // 2, head % 2
    xl, y, z = loop // 32, (loop // 8) % 4, loop % 8
    guest = c != xl

    def device(xh_=xh, c_=c, xl_=xl, y_=y, z_=z):
        return (xh_ * 2 + c_, (xl_ * 4 + y_) * 8 + z_)

    sibling = device(c_=1 - c)
    partner = device(c_=1 - c, xl_=1 - xl)
    across = device(xh_=1 - xh)
    up, down = device(y_=(y + 1) % 4), device(y_=(y + 3) % 4)
    along = {k: device(z_=(z + k + 8) % 8) for k in (1, -1, 2, -2, 3, -3, 4)}

    started = []

    def remote(src, dst, to):
        n = len(started)
        copy = pltpu.make_async_remote_copy(
            src_ref=src, dst_ref=dst, send_sem=send_sem.at[n], recv_sem=recv_sem.at[n],
            device_id=to, device_id_type=MESH,
        )
        started.append(copy)
        return copy

    def send(src, dst, to):
        copy = remote(src, dst, to)
        copy.start()
        return copy

    weight_copies = []
    for j, (d, e) in enumerate(((0, 0), (1, 0), (0, 1), (1, 1))):
        block = (xh + d) % 2 * 2 + (c + e) % 2
        weight_copies.append(pltpu.make_async_copy(
            weight.at[:, pl.ds(pl.multiple_of(block * 1280, 1280), 1280)], wv.at[j], local_sem.at[j]))

    moves = (
        (pk, kv.at[0, 0, 0, 0]),
        (pv, kv.at[1, 0, 0, 0]),
        (tk, tkv.at[0, pl.ds(0, 64)]),
        (tv, tkv.at[1, pl.ds(0, 64)]),
        (pq, q.at[pl.ds(0, 128)]),
        (tq, q.at[pl.ds(128, 64)]),
    )
    here = [pltpu.make_async_copy(s, d, local_sem.at[4 + i]) for i, (s, d) in enumerate(moves)]
    there = [remote(s, d, partner) for s, d in moves]

    barrier = pltpu.get_barrier_semaphore()
    friends = [sibling, partner, across, up, down] + list(along.values())
    for friend in friends:
        pl.semaphore_signal(barrier, inc=1, device_id=friend, device_id_type=MESH)

    @pl.when(jnp.logical_not(guest))
    def _():
        for copy in here:
            copy.start()

    for copy in weight_copies:
        copy.start()

    row = lax.broadcasted_iota(jnp.int32, (128, 128), 0)
    col = lax.broadcasted_iota(jnp.int32, (128, 128), 1)
    shifted = col - (row >= 64).astype(jnp.int32)
    for i, dy in enumerate(LINES):
        for p, dz in enumerate(STEPS):
            for rr in range(2):
                r = (c + rr) % 2
                block = 2 * ((r * 4 + (y + dy + 4) % 4) * 8 + (z + dz + 8) % 8)
                hot[i, p, rr] = jnp.where(shifted == block, 1.0, 0.0).astype(BF16)

    tkv[:, pl.ds(64, 64), :] = jnp.zeros((2, 64, 128), BF16)

    lane = lax.broadcasted_iota(jnp.int32, (1, 128), 1)
    first = 2 * ((c * 4 + y) * 8 + z)
    ranks = order[...]
    for g in range(3):
        if g < 2:
            own = jnp.sum(jnp.where(lane == first + g, ranks, 0), axis=1, keepdims=True)
            seen = jnp.where(ranks < own, 0.0, HIDDEN)
        else:
            seen = jnp.zeros((1, 128), F32)
        for h in range(2):
            qs[2 * g + h, :, 128:] = jnp.broadcast_to(seen, (256, 128)).astype(BF16)

    pl.semaphore_wait(barrier, len(friends))

    @pl.when(guest)
    def _():
        for copy in there:
            copy.start()

    def arrived(numbers):
        @pl.when(guest)
        def _():
            for n in numbers:
                there[n].wait_recv()

        @pl.when(jnp.logical_not(guest))
        def _():
            for n in numbers:
                here[n].wait()

    arrived((0, 1))

    def shards(i, batch, rr, part=None):
        lo, hi = BATCHES[batch]
        part = slice(None) if part is None else part
        return kv.at[part, i, pl.ds(lo, hi - lo), rr]

    sib, ups, downs, far = {}, {}, {}, {}

    def to_sibling(i, b):
        sib[i, b] = send(shards(i, b, 0), shards(i, b, 1), sibling)

    def to_lines(b):
        ups[b] = send(shards(0, b, 0), shards(2, b, 0), up)
        downs[b] = send(shards(0, b, 0), shards(1, b, 0), down)

    def pass_on(b):
        far[0, b] = send(shards(1, b, 0, 0), shards(3, b, 0, 0), down)
        far[1, b] = send(shards(2, b, 0, 1), shards(3, b, 0, 1), up)

    zs = {}

    def to_z(k):
        zs[k] = send(kv.at[:, 0, 0, 0], kv.at[:, 0, PLACE[-k], 0], along[k])

    to_z(1)
    to_z(-1)
    to_sibling(0, 0)
    to_lines(0)
    for k in (2, -2, 3, -3, 4):
        to_z(k)

    arrived((2, 3, 4, 5))
    for t in range(6):
        g, h = t // 2, t % 2
        for e in range(4):
            qs[t, e * 64:(e + 1) * 64, :128] = q[g * 64:(g + 1) * 64, (h * 4 + e) * 128:(h * 4 + e + 1) * 128]

    ones = jnp.ones((128, 128), BF16)
    slot = lax.broadcasted_iota(jnp.int32, (256, 128), 0) % 64
    key = lax.broadcasted_iota(jnp.int32, (256, 128), 1)
    early = (key < 64) & (key <= slot)
    late = (key >= 64) & (key - 64 <= slot)
    for t in range(6):
        g = t // 2
        keys, values = (kv[0, 0, 0, 0], kv[1, 0, 0, 0]) if g < 2 else (tkv[0], tkv[1])
        s = lax.dot_general(qs[t, :, :128], keys, NT, preferred_element_type=F32)
        s = jnp.where(late if g == 1 else early, s, HIDDEN)
        peak = jnp.max(s, axis=1, keepdims=True)
        w = jnp.exp2((s - peak) * RATE).astype(BF16)
        acc[t] = jnp.dot(w, jnp.concatenate([values, ones], axis=1), preferred_element_type=F32)
        top[t] = jnp.broadcast_to(peak, (256, 128))

    def attend(i, lo, hi, t):
        n = (hi - lo) * 256
        keys = kv[0, i, lo:hi].reshape(n, 128)
        values = kv[1, i, lo:hi].reshape(n, 128)
        marks = hot[i, lo:hi].reshape(n, 128)
        s = lax.dot_general(
            qs[t], jnp.concatenate([keys, marks], axis=1), NT, preferred_element_type=F32)
        old = top[t]
        new = jnp.maximum(old, jnp.max(s, axis=1, keepdims=True))
        w = jnp.exp2((s - new[:, :1]) * RATE).astype(BF16)
        shrink = jnp.exp2((old - new) * RATE)
        top[t] = new
        add = jnp.dot(
            w, jnp.concatenate([values, jnp.ones((n, 128), BF16)], axis=1), preferred_element_type=F32)
        acc[t] = acc[t] * shrink[:, :1] + add

    def attend_all(i, lo, hi):
        @pl.loop(0, 3)
        def _(g):
            for h in range(2):
                attend(i, lo, hi, 2 * g + h)

    zs[1].wait_recv()
    zs[-1].wait_recv()
    to_lines(1)
    to_sibling(0, 1)
    sib[0, 0].wait_recv()
    zs[2].wait_recv()
    zs[-2].wait_recv()
    to_lines(2)
    to_sibling(0, 2)
    sib[0, 1].wait_recv()
    attend_all(0, 0, 3)
    for b in (0, 1):
        ups[b].wait_recv()
        downs[b].wait_recv()
        pass_on(b)
        to_sibling(1, b)
        to_sibling(2, b)
    sib[0, 2].wait_recv()
    attend_all(0, 3, 5)
    for k in (3, -3, 4):
        zs[k].wait_recv()
    to_lines(3)
    to_sibling(0, 3)
    ups[2].wait_recv()
    downs[2].wait_recv()
    pass_on(2)
    to_sibling(1, 2)
    to_sibling(2, 2)
    sib[0, 3].wait_recv()
    attend_all(0, 5, 8)
    for b in (0, 1, 2):
        sib[1, b].wait_recv()
    attend_all(1, 0, 5)
    for b in (0, 1, 2):
        far[0, b].wait_recv()
        far[1, b].wait_recv()
        to_sibling(3, b)
    ups[3].wait_recv()
    downs[3].wait_recv()
    pass_on(3)
    to_sibling(1, 3)
    to_sibling(2, 3)
    for b in (0, 1, 2):
        sib[2, b].wait_recv()
    attend_all(2, 0, 5)
    far[0, 3].wait_recv()
    far[1, 3].wait_recv()
    to_sibling(3, 3)
    for i in (1, 2):
        sib[i, 3].wait_recv()
    for b in range(4):
        sib[3, b].wait_recv()

    for copy in weight_copies:
        copy.wait()

    back, core, over = {}, {}, {}

    def finish(g):
        for h in range(2):
            t = 2 * g + h
            attend(1, 5, 8, t)
            attend(2, 5, 8, t)
            attend(3, 0, 8, t)
            out = (acc[t, :, :128] / acc[t, :, 128:]).astype(BF16)
            for e in range(4):
                mixed[g, h, :, e * 128:(e + 1) * 128] = out[e * 64:(e + 1) * 64]
            back[g, h] = remote(mixed.at[g, h], mine.at[g, h], partner)

            @pl.when(guest)
            def _():
                back[g, h].start()

            @pl.when(jnp.logical_not(guest))
            def _():
                mine[g, h] = mixed[g, h]

    def project(g):
        @pl.when(guest)
        def _():
            for h in range(2):
                back[g, h].wait_recv()

        lefts, rights = mine[g, 0], mine[g, 1]
        if g == 2:
            live = lax.broadcasted_iota(jnp.int32, (64, 512), 0) < tail_len[0]
            lefts = jnp.where(live, lefts, jnp.zeros_like(lefts))
            rights = jnp.where(live, rights, jnp.zeros_like(rights))
        rows = jnp.concatenate([lefts, rights], axis=1)
        for j in (3, 2, 1, 0):
            for n in range(5):
                part = jnp.dot(rows, wv[j, :, n * 256:(n + 1) * 256], preferred_element_type=F32)
                if j >= 2:
                    half_out[g, j - 2, :, n * 256:(n + 1) * 256] = part.astype(BF16)
                else:
                    kept[g, j, :, n * 256:(n + 1) * 256] = part
            if j == 2:
                core[g] = send(half_out.at[g], half_in.at[g], sibling)

    def cross(g):
        core[g].wait_recv()
        cross_out[g] = (kept[g, 1] + half_in[g, 1].astype(F32)).astype(BF16)
        over[g] = send(cross_out.at[g], cross_in.at[g], across)

    def close(g):
        over[g].wait_recv()
        out = kept[g, 0] + half_in[g, 0].astype(F32) + cross_in[g].astype(F32)
        if g < 2:
            prompt_out[g * 64:(g + 1) * 64] = out.astype(BF16)
        else:
            tail_out[...] = out.astype(BF16)

    finish(0)
    finish(1)
    project(0)
    finish(2)
    cross(0)
    project(1)
    cross(1)
    project(2)
    cross(2)
    close(0)
    close(1)
    close(2)

    lone = list(there) + list(back.values())
    for copy in started:
        if not any(copy is other for other in lone):
            copy.wait_send()

    @pl.when(guest)
    def _():
        for copy in lone:
            copy.wait_send()


COPIES = 6 + 7 + 16 + 8 + 8 + 6 + 3 + 3


def on_device(pq, pk, pv, tq, tk, tv, tail_len, order, weight):
    vmem, hbm = pl.BlockSpec(memory_space=pltpu.VMEM), pl.BlockSpec(memory_space=pl.ANY)
    prompt, tail = pl.pallas_call(
        kernel,
        out_shape=(jax.ShapeDtypeStruct((128, 1280), BF16), jax.ShapeDtypeStruct((64, 1280), BF16)),
        in_specs=[hbm] * 6 + [pl.BlockSpec(memory_space=pltpu.SMEM), vmem, hbm],
        out_specs=(vmem, vmem),
        scratch_shapes=[
            pltpu.VMEM((2, 4, 8, 2, 128, 128), BF16),
            pltpu.VMEM((192, 1024), BF16),
            pltpu.VMEM((2, 128, 128), BF16),
            pltpu.VMEM((4, 8, 2, 128, 128), BF16),
            pltpu.VMEM((4, 1024, 1280), BF16),
            pltpu.VMEM((6, 256, 256), BF16),
            pltpu.VMEM((6, 256, 256), F32),
            pltpu.VMEM((6, 256, 128), F32),
            pltpu.VMEM((3, 2, 64, 512), BF16),
            pltpu.VMEM((3, 2, 64, 512), BF16),
            pltpu.VMEM((3, 2, 64, 1280), BF16),
            pltpu.VMEM((3, 2, 64, 1280), BF16),
            pltpu.VMEM((3, 2, 64, 1280), F32),
            pltpu.VMEM((3, 64, 1280), BF16),
            pltpu.VMEM((3, 64, 1280), BF16),
            pltpu.SemaphoreType.DMA((COPIES,)),
            pltpu.SemaphoreType.DMA((COPIES,)),
            pltpu.SemaphoreType.DMA((10,)),
        ],
        compiler_params=pltpu.CompilerParams(
            collective_id=0, has_side_effects=True, vmem_limit_bytes=56 << 20
        ),
    )(pq, pk, pv, tq.reshape(64, 1024), tk.reshape(64, 128), tv.reshape(64, 128),
      tail_len, order.reshape(1, 128), weight)
    return prompt, tail.reshape(1, 64, 1280)


def solution(mesh):
    placed = (
        P("loop", "head"),
        P("loop", "head"),
        P("loop", "head"),
        P("loop", None, "head"),
        P("loop", None, "head"),
        P("loop", None, "head"),
        P("loop"),
        P(),
        P("head", None),
    )
    return jax.shard_map(
        on_device,
        mesh=mesh,
        in_specs=placed,
        out_specs=(P("loop", "head"), P("loop", None, "head")),
        check_vma=False,
    )
```

```python
import functools
import math

import jax
import jax.numpy as jnp
from jax import lax
from jax.experimental import pallas as pl
from jax.experimental.pallas import tpu as pltpu
from jax.sharding import PartitionSpec as P

F32, BF16 = jnp.float32, jnp.bfloat16
MESH = pl.DeviceIdType.MESH
NT = (((1,), (1,)), ((), ()))
HIDDEN = -1e30
RATE = math.log2(math.e) / math.sqrt(128.0)
STEPS = (0, 1, -1, 2, -2, 3, -3, 4)
PLACE = {0: 0, 1: 1, -1: 2, 2: 3, -2: 4, 3: 5, -3: 6, 4: 7, -4: 7}
BATCHES = ((0, 1), (1, 3), (3, 5), (5, 7), (7, 8))
LINES = (0, 1, -1, 2)


def kernel(
    pq, pk, pv, tq, tk, tv, tail_len, order, weight,
    prompt_out, tail_out,
    kv, q, tkv, hot, wv, qs, acc, top, mixed, mine, half_out, half_in, kept, cross_out, cross_in,
    send_sem, recv_sem, local_sem,
):
    head, loop = lax.axis_index("head"), lax.axis_index("loop")
    xh, c = head // 2, head % 2
    xl, y, z = loop // 32, (loop // 8) % 4, loop % 8
    guest = c != xl

    def device(xh_=xh, c_=c, xl_=xl, y_=y, z_=z):
        return (xh_ * 2 + c_, (xl_ * 4 + y_) * 8 + z_)

    sibling = device(c_=1 - c)
    partner = device(c_=1 - c, xl_=1 - xl)
    across = device(xh_=1 - xh)
    up, down = device(y_=(y + 1) % 4), device(y_=(y + 3) % 4)
    along = {k: device(z_=(z + k + 8) % 8) for k in (1, -1, 2, -2)}
    beyond = device(y_=(y + 2) % 4)

    started = []

    def remote(src, dst, to):
        n = len(started)
        copy = pltpu.make_async_remote_copy(
            src_ref=src, dst_ref=dst, send_sem=send_sem.at[n], recv_sem=recv_sem.at[n],
            device_id=to, device_id_type=MESH,
        )
        started.append(copy)
        return copy

    def send(src, dst, to):
        copy = remote(src, dst, to)
        copy.start()
        return copy

    weight_copies = []
    for j, (d, e) in enumerate(((0, 0), (1, 0), (0, 1), (1, 1))):
        block = (xh + d) % 2 * 2 + (c + e) % 2
        weight_copies.append(pltpu.make_async_copy(
            weight.at[:, pl.ds(pl.multiple_of(block * 1280, 1280), 1280)], wv.at[j], local_sem.at[j]))

    moves = (
        (pk, kv.at[0, 0, 0, 0]),
        (pv, kv.at[1, 0, 0, 0]),
        (tk, tkv.at[0, pl.ds(0, 64)]),
        (tv, tkv.at[1, pl.ds(0, 64)]),
        (tq, q.at[pl.ds(128, 64)]),
        (pq.at[pl.ds(0, 64)], q.at[pl.ds(0, 64)]),
        (pq.at[pl.ds(64, 64)], q.at[pl.ds(64, 64)]),
    )
    here = [pltpu.make_async_copy(s, d, local_sem.at[4 + i]) for i, (s, d) in enumerate(moves)]
    there = [remote(s, d, partner) for s, d in moves]

    barrier = pltpu.get_barrier_semaphore()
    friends = [sibling, partner, across, up, down, beyond] + list(along.values())
    for friend in friends:
        pl.semaphore_signal(barrier, inc=1, device_id=friend, device_id_type=MESH)

    @pl.when(jnp.logical_not(guest))
    def _():
        for copy in here:
            copy.start()

    for copy in weight_copies:
        copy.start()

    row = lax.broadcasted_iota(jnp.int32, (128, 128), 0)
    col = lax.broadcasted_iota(jnp.int32, (128, 128), 1)
    shifted = col - (row >= 64).astype(jnp.int32)
    for i, dy in enumerate(LINES):
        for p, dz in enumerate(STEPS):
            for rr in range(2):
                r = (c + rr) % 2
                block = 2 * ((r * 4 + (y + dy + 4) % 4) * 8 + (z + dz + 8) % 8)
                hot[i, p, rr] = jnp.where(shifted == block, 1.0, 0.0).astype(BF16)

    tkv[:, pl.ds(64, 64), :] = jnp.zeros((2, 64, 128), BF16)

    lane = lax.broadcasted_iota(jnp.int32, (1, 128), 1)
    first = 2 * ((c * 4 + y) * 8 + z)
    ranks = order[...]
    for g in range(3):
        if g < 2:
            own = jnp.sum(jnp.where(lane == first + g, ranks, 0), axis=1, keepdims=True)
            seen = jnp.where(ranks < own, 0.0, HIDDEN)
        else:
            seen = jnp.zeros((1, 128), F32)
        for h in range(2):
            qs[2 * g + h, :, 128:] = jnp.broadcast_to(seen, (256, 128)).astype(BF16)

    pl.semaphore_wait(barrier, len(friends))

    @pl.when(guest)
    def _():
        for copy in there:
            copy.start()

    def arrived(numbers):
        @pl.when(guest)
        def _():
            for n in numbers:
                there[n].wait_recv()

        @pl.when(jnp.logical_not(guest))
        def _():
            for n in numbers:
                here[n].wait()

    arrived((0, 1))

    def shards(i, batch, rr, part=None):
        lo, hi = BATCHES[batch]
        part = slice(None) if part is None else part
        return kv.at[part, i, pl.ds(lo, hi - lo), rr]

    sib, ups, downs, zs = {}, {}, {}, {}

    def to_sibling(i, b):
        sib[i, b] = send(shards(i, b, 0), shards(i, b, 1), sibling)

    def to_lines(b):
        ups[b] = send(shards(0, b, 0), shards(2, b, 0), up)
        downs[b] = send(shards(0, b, 0), shards(1, b, 0), down)

    def to_z(i, k):
        zs[i, k] = send(kv.at[:, i, 0, 0], kv.at[:, i, PLACE[-k], 0], along[k])

    def pass_on(i):
        for k in (1, -1):
            come = PLACE[-2 * k]
            zs[i, 3 * k] = send(kv.at[:, i, come, 0], kv.at[:, i, PLACE[-3 * k], 0], along[k])
        for k in (1, -1):
            come, part = PLACE[-2 * k], (1 - k) // 2
            zs[i, 4 * k] = send(kv.at[part, i, come, 0], kv.at[part, i, 7, 0], along[2 * k])

    def got_z(i, *ks):
        for k in ks:
            zs[i, k].wait_recv()
            zs[i, -k].wait_recv()

    def got_lines(b):
        ups[b].wait_recv()
        downs[b].wait_recv()
        to_sibling(1, b)
        to_sibling(2, b)

    def got_sibling(i, *bs):
        for b in bs:
            sib[i, b].wait_recv()

    to_z(0, 1)
    to_z(0, -1)
    to_sibling(0, 0)
    to_lines(0)
    own_far = send(kv.at[:, 0, 0, 0], kv.at[:, 3, 0, 0], beyond)
    to_z(0, 2)
    to_z(0, -2)

    ones = jnp.ones((128, 128), BF16)
    slot = lax.broadcasted_iota(jnp.int32, (256, 128), 0) % 64
    key = lax.broadcasted_iota(jnp.int32, (256, 128), 1)
    early = (key < 64) & (key <= slot)
    late = (key >= 64) & (key - 64 <= slot)

    def begin(g):
        for h in range(2):
            t = 2 * g + h
            for e in range(4):
                qs[t, e * 64:(e + 1) * 64, :128] = q[g * 64:(g + 1) * 64, (h * 4 + e) * 128:(h * 4 + e + 1) * 128]
            keys, values = (kv[0, 0, 0, 0], kv[1, 0, 0, 0]) if g < 2 else (tkv[0], tkv[1])
            s = lax.dot_general(qs[t, :, :128], keys, NT, preferred_element_type=F32)
            s = jnp.where(late if g == 1 else early, s, HIDDEN)
            peak = jnp.max(s, axis=1, keepdims=True)
            w = jnp.exp2((s - peak) * RATE).astype(BF16)
            acc[t] = jnp.dot(w, jnp.concatenate([values, ones], axis=1), preferred_element_type=F32)
            top[t] = jnp.broadcast_to(peak, (256, 128))

    def scores(i, lo, hi, t):
        n = (hi - lo) * 256
        keys = kv[0, i, lo:hi].reshape(n, 128)
        marks = hot[i, lo:hi].reshape(n, 128)
        return lax.dot_general(
            qs[t], jnp.concatenate([keys, marks], axis=1), NT, preferred_element_type=F32)

    def attend(steps):
        ready = scores(*steps[0])
        for at, (i, lo, hi, t) in enumerate(steps):
            s = ready
            if at + 1 < len(steps):
                ready = scores(*steps[at + 1])
            n = (hi - lo) * 256
            values = kv[1, i, lo:hi].reshape(n, 128)
            old = top[t]
            new = jnp.maximum(old, jnp.max(s, axis=1, keepdims=True))
            w = jnp.exp2((s - new[:, :1]) * RATE).astype(BF16)
            shrink = jnp.exp2((old - new) * RATE)
            top[t] = new
            add = jnp.dot(
                w, jnp.concatenate([values, jnp.ones((n, 128), BF16)], axis=1), preferred_element_type=F32)
            acc[t] = acc[t] * shrink[:, :1] + add

    def attend_all(i, lo, hi):
        attend([(i, lo, hi, t) for t in range(6)])

    arrived((2, 3, 4))
    begin(2)
    got_z(0, 1)
    to_lines(1)
    to_sibling(0, 1)
    own_far.wait_recv()
    for k in (1, -1, 2, -2):
        to_z(3, k)
    to_sibling(3, 0)
    arrived((5,))
    begin(0)
    arrived((6,))
    begin(1)
    got_z(0, 2)
    pass_on(0)
    to_lines(2)
    to_sibling(0, 2)
    got_lines(0)
    got_lines(1)
    got_sibling(0, 0, 1)
    attend_all(0, 0, 3)
    got_z(3, 1)
    to_sibling(3, 1)
    got_z(0, 3)
    to_lines(3)
    to_sibling(0, 3)
    got_z(3, 2)
    pass_on(3)
    to_sibling(3, 2)
    got_z(0, 4)
    to_lines(4)
    to_sibling(0, 4)
    got_lines(2)
    got_sibling(1, 0, 1, 2)
    attend_all(1, 0, 5)
    got_lines(3)
    got_z(3, 3)
    to_sibling(3, 3)
    got_sibling(2, 0, 1, 2)
    attend_all(2, 0, 5)
    got_lines(4)
    got_z(3, 4)
    to_sibling(3, 4)
    got_sibling(0, 2, 3, 4)
    attend_all(0, 3, 8)
    got_sibling(3, 0, 1, 2)
    attend_all(3, 0, 5)
    for i in (1, 2):
        got_sibling(i, 3, 4)
    got_sibling(3, 3, 4)

    for copy in weight_copies:
        copy.wait()

    back, core, over = {}, {}, {}

    def finish(g):
        attend([(i, lo, hi, 2 * g + h) for i, lo, hi in ((1, 5, 8), (2, 5, 8), (3, 5, 8)) for h in range(2)])
        for h in range(2):
            t = 2 * g + h
            out = (acc[t, :, :128] / acc[t, :, 128:]).astype(BF16)
            for e in range(4):
                mixed[g, h, :, e * 128:(e + 1) * 128] = out[e * 64:(e + 1) * 64]
            back[g, h] = remote(mixed.at[g, h], mine.at[g, h], partner)

            @pl.when(guest)
            def _():
                back[g, h].start()

            @pl.when(jnp.logical_not(guest))
            def _():
                mine[g, h] = mixed[g, h]

    def project(g):
        @pl.when(guest)
        def _():
            for h in range(2):
                back[g, h].wait_recv()

        lefts, rights = mine[g, 0], mine[g, 1]
        if g == 2:
            live = lax.broadcasted_iota(jnp.int32, (64, 512), 0) < tail_len[0]
            lefts = jnp.where(live, lefts, jnp.zeros_like(lefts))
            rights = jnp.where(live, rights, jnp.zeros_like(rights))
        rows = jnp.concatenate([lefts, rights], axis=1)
        for j in (3, 2, 1, 0):
            for n in range(5):
                part = jnp.dot(rows, wv[j, :, n * 256:(n + 1) * 256], preferred_element_type=F32)
                if j >= 2:
                    half_out[g, j - 2, :, n * 256:(n + 1) * 256] = part.astype(BF16)
                else:
                    kept[g, j, :, n * 256:(n + 1) * 256] = part
            if j == 2:
                core[g] = send(half_out.at[g], half_in.at[g], sibling)

    def cross(g):
        core[g].wait_recv()
        cross_out[g] = (kept[g, 1] + half_in[g, 1].astype(F32)).astype(BF16)
        over[g] = send(cross_out.at[g], cross_in.at[g], across)

    def close(g):
        over[g].wait_recv()
        out = kept[g, 0] + half_in[g, 0].astype(F32) + cross_in[g].astype(F32)
        if g < 2:
            prompt_out[g * 64:(g + 1) * 64] = out.astype(BF16)
        else:
            tail_out[...] = out.astype(BF16)

    finish(0)
    finish(1)
    project(0)
    finish(2)
    cross(0)
    project(1)
    cross(1)
    project(2)
    cross(2)
    close(0)
    close(1)
    close(2)

    lone = list(there) + list(back.values())
    for copy in started:
        if not any(copy is other for other in lone):
            copy.wait_send()

    @pl.when(guest)
    def _():
        for copy in lone:
            copy.wait_send()


COPIES = 7 + 8 + 8 + 1 + 10 + 20 + 6 + 3 + 3


def hand_over(prompt, tail, prompt_out, tail_out):
    prompt_out[...] = prompt[...]
    tail_out[...] = tail[...]


def on_device(pq, pk, pv, tq, tk, tv, tail_len, order, weight):
    vmem, hbm = pl.BlockSpec(memory_space=pltpu.VMEM), pl.BlockSpec(memory_space=pl.ANY)
    prompt, tail = pl.pallas_call(
        kernel,
        out_shape=(jax.ShapeDtypeStruct((128, 1280), BF16), jax.ShapeDtypeStruct((64, 1280), BF16)),
        in_specs=[hbm] * 6 + [pl.BlockSpec(memory_space=pltpu.SMEM), vmem, hbm],
        out_specs=(vmem, vmem),
        scratch_shapes=[
            pltpu.VMEM((2, 4, 8, 2, 128, 128), BF16),
            pltpu.VMEM((192, 1024), BF16),
            pltpu.VMEM((2, 128, 128), BF16),
            pltpu.VMEM((4, 8, 2, 128, 128), BF16),
            pltpu.VMEM((4, 1024, 1280), BF16),
            pltpu.VMEM((6, 256, 256), BF16),
            pltpu.VMEM((6, 256, 256), F32),
            pltpu.VMEM((6, 256, 128), F32),
            pltpu.VMEM((3, 2, 64, 512), BF16),
            pltpu.VMEM((3, 2, 64, 512), BF16),
            pltpu.VMEM((3, 2, 64, 1280), BF16),
            pltpu.VMEM((3, 2, 64, 1280), BF16),
            pltpu.VMEM((3, 2, 64, 1280), F32),
            pltpu.VMEM((3, 64, 1280), BF16),
            pltpu.VMEM((3, 64, 1280), BF16),
            pltpu.SemaphoreType.DMA((COPIES,)),
            pltpu.SemaphoreType.DMA((COPIES,)),
            pltpu.SemaphoreType.DMA((11,)),
        ],
        compiler_params=pltpu.CompilerParams(
            collective_id=0, has_side_effects=True, vmem_limit_bytes=56 << 20
        ),
    )(pq, pk, pv, tq.reshape(64, 1024), tk.reshape(64, 128), tv.reshape(64, 128),
      tail_len, order.reshape(1, 128), weight)
    return pl.pallas_call(
        hand_over,
        out_shape=(jax.ShapeDtypeStruct((128, 1280), BF16), jax.ShapeDtypeStruct((1, 64, 1280), BF16)),
        in_specs=[vmem, vmem],
        out_specs=(vmem, vmem),
    )(prompt, tail.reshape(1, 64, 1280))


def solution(mesh):
    placed = (
        P("loop", "head"),
        P("loop", "head"),
        P("loop", "head"),
        P("loop", None, "head"),
        P("loop", None, "head"),
        P("loop", None, "head"),
        P("loop"),
        P(),
        P("head", None),
    )
    return jax.shard_map(
        on_device,
        mesh=mesh,
        in_specs=placed,
        out_specs=(P("loop", "head"), P("loop", None, "head")),
        check_vma=False,
    )
```

```python
import functools
import math

import jax
import jax.numpy as jnp
from jax import lax
from jax.experimental import pallas as pl
from jax.experimental.pallas import tpu as pltpu
from jax.sharding import PartitionSpec as P

F32, BF16 = jnp.float32, jnp.bfloat16
MESH = pl.DeviceIdType.MESH
NT = (((1,), (1,)), ((), ()))
HIDDEN = -1e30
RATE = math.log2(math.e) / math.sqrt(128.0)
STEPS = (0, 1, -1, 2, -2, 3, -3, 4)
PLACE = {0: 0, 1: 1, -1: 2, 2: 3, -2: 4, 3: 5, -3: 6, 4: 7, -4: 7}
BATCHES = ((0, 1), (1, 3), (3, 5), (5, 7), (7, 8))
LINES = (0, 1, -1, 2)


def kernel(
    pq, pk, pv, tq, tk, tv, tail_len, order, weight,
    prompt_out, tail_out,
    kv, q, tkv, hot, wv, qs, acc, top, mixed, mine, half_out, half_in, kept, cross_out, cross_in,
    send_sem, recv_sem, local_sem,
):
    head, loop = lax.axis_index("head"), lax.axis_index("loop")
    xh, c = head // 2, head % 2
    xl, y, z = loop // 32, (loop // 8) % 4, loop % 8
    guest = c != xl

    def device(xh_=xh, c_=c, xl_=xl, y_=y, z_=z):
        return (xh_ * 2 + c_, (xl_ * 4 + y_) * 8 + z_)

    sibling = device(c_=1 - c)
    partner = device(c_=1 - c, xl_=1 - xl)
    across = device(xh_=1 - xh)
    up, down = device(y_=(y + 1) % 4), device(y_=(y + 3) % 4)
    along = {k: device(z_=(z + k + 8) % 8) for k in (1, -1, 2, -2)}
    beyond = device(y_=(y + 2) % 4)

    started = []

    def remote(src, dst, to):
        n = len(started)
        copy = pltpu.make_async_remote_copy(
            src_ref=src, dst_ref=dst, send_sem=send_sem.at[n], recv_sem=recv_sem.at[n],
            device_id=to, device_id_type=MESH,
        )
        started.append(copy)
        return copy

    def send(src, dst, to):
        copy = remote(src, dst, to)
        copy.start()
        return copy

    weight_copies = []
    for j, (d, e) in enumerate(((0, 0), (1, 0), (0, 1), (1, 1))):
        block = (xh + d) % 2 * 2 + (c + e) % 2
        weight_copies.append(pltpu.make_async_copy(
            weight.at[:, pl.ds(pl.multiple_of(block * 1280, 1280), 1280)], wv.at[j], local_sem.at[j]))

    moves = (
        (pk, kv.at[0, 0, 0, 0]),
        (pv, kv.at[1, 0, 0, 0]),
        (tk, tkv.at[0, pl.ds(0, 64)]),
        (tv, tkv.at[1, pl.ds(0, 64)]),
        (tq, q.at[pl.ds(128, 64)]),
        (pq.at[pl.ds(0, 64)], q.at[pl.ds(0, 64)]),
        (pq.at[pl.ds(64, 64)], q.at[pl.ds(64, 64)]),
    )
    here = [pltpu.make_async_copy(s, d, local_sem.at[4 + i]) for i, (s, d) in enumerate(moves)]
    there = [remote(s, d, partner) for s, d in moves]

    barrier = pltpu.get_barrier_semaphore()
    friends = [sibling, partner, across, up, down, beyond] + list(along.values())
    for friend in friends:
        pl.semaphore_signal(barrier, inc=1, device_id=friend, device_id_type=MESH)

    @pl.when(jnp.logical_not(guest))
    def _():
        for copy in here:
            copy.start()

    for copy in weight_copies:
        copy.start()

    row = lax.broadcasted_iota(jnp.int32, (128, 128), 0)
    col = lax.broadcasted_iota(jnp.int32, (128, 128), 1)
    shifted = col - (row >= 64).astype(jnp.int32)
    for i, dy in enumerate(LINES):
        for p, dz in enumerate(STEPS):
            for rr in range(2):
                r = (c + rr) % 2
                block = 2 * ((r * 4 + (y + dy + 4) % 4) * 8 + (z + dz + 8) % 8)
                hot[i, p, rr] = jnp.where(shifted == block, 1.0, 0.0).astype(BF16)

    tkv[:, pl.ds(64, 64), :] = jnp.zeros((2, 64, 128), BF16)

    lane = lax.broadcasted_iota(jnp.int32, (1, 128), 1)
    first = 2 * ((c * 4 + y) * 8 + z)
    ranks = order[...]
    for g in range(3):
        if g < 2:
            own = jnp.sum(jnp.where(lane == first + g, ranks, 0), axis=1, keepdims=True)
            seen = jnp.where(ranks < own, 0.0, HIDDEN)
        else:
            seen = jnp.zeros((1, 128), F32)
        for h in range(2):
            qs[2 * g + h, :, 128:] = jnp.broadcast_to(seen, (256, 128)).astype(BF16)

    pl.semaphore_wait(barrier, len(friends))

    @pl.when(guest)
    def _():
        for copy in there:
            copy.start()

    def arrived(numbers):
        @pl.when(guest)
        def _():
            for n in numbers:
                there[n].wait_recv()

        @pl.when(jnp.logical_not(guest))
        def _():
            for n in numbers:
                here[n].wait()

    arrived((0, 1))

    def shards(i, batch, rr, part=None):
        lo, hi = BATCHES[batch]
        part = slice(None) if part is None else part
        return kv.at[part, i, pl.ds(lo, hi - lo), rr]

    sib, ups, downs, zs = {}, {}, {}, {}

    def to_sibling(i, b):
        sib[i, b] = send(shards(i, b, 0), shards(i, b, 1), sibling)

    def to_lines(b):
        ups[b] = send(shards(0, b, 0), shards(2, b, 0), up)
        downs[b] = send(shards(0, b, 0), shards(1, b, 0), down)

    def to_z(i, k):
        zs[i, k] = send(kv.at[:, i, 0, 0], kv.at[:, i, PLACE[-k], 0], along[k])

    def pass_on(i):
        for k in (1, -1):
            come = PLACE[-2 * k]
            zs[i, 3 * k] = send(kv.at[:, i, come, 0], kv.at[:, i, PLACE[-3 * k], 0], along[k])
        for k in (1, -1):
            come, part = PLACE[-2 * k], (1 - k) // 2
            zs[i, 4 * k] = send(kv.at[part, i, come, 0], kv.at[part, i, 7, 0], along[2 * k])

    def got_z(i, *ks):
        for k in ks:
            zs[i, k].wait_recv()
            zs[i, -k].wait_recv()

    def got_lines(b):
        ups[b].wait_recv()
        downs[b].wait_recv()
        to_sibling(1, b)
        to_sibling(2, b)

    def got_sibling(i, *bs):
        for b in bs:
            sib[i, b].wait_recv()

    to_z(0, 1)
    to_z(0, -1)
    to_sibling(0, 0)
    to_lines(0)
    own_far = send(kv.at[:, 0, 0, 0], kv.at[:, 3, 0, 0], beyond)
    to_z(0, 2)
    to_z(0, -2)

    ones = jnp.ones((128, 128), BF16)
    slot = lax.broadcasted_iota(jnp.int32, (256, 128), 0) % 64
    key = lax.broadcasted_iota(jnp.int32, (256, 128), 1)
    early = (key < 64) & (key <= slot)
    late = (key >= 64) & (key - 64 <= slot)

    def begin(g):
        for h in range(2):
            t = 2 * g + h
            for e in range(4):
                qs[t, e * 64:(e + 1) * 64, :128] = q[g * 64:(g + 1) * 64, (h * 4 + e) * 128:(h * 4 + e + 1) * 128]
            keys, values = (kv[0, 0, 0, 0], kv[1, 0, 0, 0]) if g < 2 else (tkv[0], tkv[1])
            s = lax.dot_general(qs[t, :, :128], keys, NT, preferred_element_type=F32)
            s = jnp.where(late if g == 1 else early, s, HIDDEN)
            peak = jnp.max(s, axis=1, keepdims=True)
            w = jnp.exp2((s - peak) * RATE).astype(BF16)
            acc[t] = jnp.dot(w, jnp.concatenate([values, ones], axis=1), preferred_element_type=F32)
            top[t] = jnp.broadcast_to(peak, (256, 128))

    def scores(i, lo, hi, t):
        n = (hi - lo) * 256
        keys = kv[0, i, lo:hi].reshape(n, 128)
        marks = hot[i, lo:hi].reshape(n, 128)
        return lax.dot_general(
            qs[t], jnp.concatenate([keys, marks], axis=1), NT, preferred_element_type=F32)

    def attend(steps):
        ready = scores(*steps[0])
        for at, (i, lo, hi, t) in enumerate(steps):
            s = ready
            if at + 1 < len(steps):
                ready = scores(*steps[at + 1])
            n = (hi - lo) * 256
            values = kv[1, i, lo:hi].reshape(n, 128)
            old = top[t]
            new = jnp.maximum(old, jnp.max(s, axis=1, keepdims=True))
            w = jnp.exp2((s - new[:, :1]) * RATE).astype(BF16)
            shrink = jnp.exp2((old - new) * RATE)
            top[t] = new
            add = jnp.dot(
                w, jnp.concatenate([values, jnp.ones((n, 128), BF16)], axis=1), preferred_element_type=F32)
            acc[t] = acc[t] * shrink[:, :1] + add

    def attend_all(i, lo, hi):
        attend([(i, lo, hi, t) for t in range(6)])

    arrived((2, 3, 4))
    begin(2)
    got_z(0, 1)
    to_lines(1)
    to_sibling(0, 1)
    own_far.wait_recv()
    for k in (1, -1, 2, -2):
        to_z(3, k)
    to_sibling(3, 0)
    arrived((5,))
    begin(0)
    arrived((6,))
    begin(1)
    got_z(0, 2)
    pass_on(0)
    to_lines(2)
    to_sibling(0, 2)
    got_lines(0)
    got_lines(1)
    got_sibling(0, 0, 1)
    attend_all(0, 0, 3)
    got_z(3, 1)
    to_sibling(3, 1)
    got_z(0, 3)
    to_lines(3)
    to_sibling(0, 3)
    got_z(3, 2)
    pass_on(3)
    to_sibling(3, 2)
    got_z(0, 4)
    to_lines(4)
    to_sibling(0, 4)
    got_lines(2)
    got_sibling(1, 0, 1, 2)
    attend_all(1, 0, 5)
    got_lines(3)
    got_z(3, 3)
    to_sibling(3, 3)
    got_sibling(2, 0, 1, 2)
    attend_all(2, 0, 5)
    got_lines(4)
    got_z(3, 4)
    to_sibling(3, 4)
    got_sibling(0, 2, 3, 4)
    attend_all(0, 3, 8)
    got_sibling(3, 0, 1, 2)
    attend_all(3, 0, 5)
    for i in (1, 2):
        got_sibling(i, 3, 4)
    got_sibling(3, 3, 4)

    for copy in weight_copies:
        copy.wait()

    back, core, over = {}, {}, {}

    def finish(g):
        attend([(i, lo, hi, 2 * g + h) for i, lo, hi in ((1, 5, 8), (2, 5, 8), (3, 5, 8)) for h in range(2)])
        for h in range(2):
            t = 2 * g + h
            out = (acc[t, :, :128] / acc[t, :, 128:]).astype(BF16)
            for e in range(4):
                mixed[g, h, :, e * 128:(e + 1) * 128] = out[e * 64:(e + 1) * 64]
            back[g, h] = remote(mixed.at[g, h], mine.at[g, h], partner)

            @pl.when(guest)
            def _():
                back[g, h].start()

            @pl.when(jnp.logical_not(guest))
            def _():
                mine[g, h] = mixed[g, h]

    def project(*groups):
        blocks = []
        for g in groups:
            @pl.when(guest)
            def _():
                for h in range(2):
                    back[g, h].wait_recv()

            block = jnp.concatenate([mine[g, 0], mine[g, 1]], axis=1)
            if g == 2:
                live = lax.broadcasted_iota(jnp.int32, (64, 1024), 0) < tail_len[0]
                block = jnp.where(live, block, jnp.zeros_like(block))
            blocks.append(block)
        rows = blocks[0] if len(blocks) == 1 else jnp.concatenate(blocks, axis=0)
        for j in (3, 2, 1, 0):
            for n in range(5):
                part = jnp.dot(rows, wv[j, :, n * 256:(n + 1) * 256], preferred_element_type=F32)
                for at, g in enumerate(groups):
                    piece = part[at * 64:(at + 1) * 64]
                    if j >= 2:
                        half_out[g, j - 2, :, n * 256:(n + 1) * 256] = piece.astype(BF16)
                    else:
                        kept[g, j, :, n * 256:(n + 1) * 256] = piece
            if j == 2:
                for g in groups:
                    core[g] = send(half_out.at[g], half_in.at[g], sibling)

    def cross(g):
        core[g].wait_recv()
        cross_out[g] = (kept[g, 1] + half_in[g, 1].astype(F32)).astype(BF16)
        over[g] = send(cross_out.at[g], cross_in.at[g], across)

    def close(g):
        over[g].wait_recv()
        out = kept[g, 0] + half_in[g, 0].astype(F32) + cross_in[g].astype(F32)
        if g < 2:
            prompt_out[g * 64:(g + 1) * 64] = out.astype(BF16)
        else:
            tail_out[...] = out.astype(BF16)

    finish(0)
    finish(1)
    finish(2)
    project(0, 1)
    cross(0)
    cross(1)
    project(2)
    cross(2)
    close(0)
    close(1)
    close(2)

    lone = list(there) + list(back.values())
    for copy in started:
        if not any(copy is other for other in lone):
            copy.wait_send()

    @pl.when(guest)
    def _():
        for copy in lone:
            copy.wait_send()


COPIES = 7 + 8 + 8 + 1 + 10 + 20 + 6 + 3 + 3


def hand_over(prompt, tail, prompt_out, tail_out):
    prompt_out[...] = prompt[...]
    tail_out[...] = tail[...]


def on_device(pq, pk, pv, tq, tk, tv, tail_len, order, weight):
    vmem, hbm = pl.BlockSpec(memory_space=pltpu.VMEM), pl.BlockSpec(memory_space=pl.ANY)
    prompt, tail = pl.pallas_call(
        kernel,
        out_shape=(jax.ShapeDtypeStruct((128, 1280), BF16), jax.ShapeDtypeStruct((64, 1280), BF16)),
        in_specs=[hbm] * 6 + [pl.BlockSpec(memory_space=pltpu.SMEM), vmem, hbm],
        out_specs=(vmem, vmem),
        scratch_shapes=[
            pltpu.VMEM((2, 4, 8, 2, 128, 128), BF16),
            pltpu.VMEM((192, 1024), BF16),
            pltpu.VMEM((2, 128, 128), BF16),
            pltpu.VMEM((4, 8, 2, 128, 128), BF16),
            pltpu.VMEM((4, 1024, 1280), BF16),
            pltpu.VMEM((6, 256, 256), BF16),
            pltpu.VMEM((6, 256, 256), F32),
            pltpu.VMEM((6, 256, 128), F32),
            pltpu.VMEM((3, 2, 64, 512), BF16),
            pltpu.VMEM((3, 2, 64, 512), BF16),
            pltpu.VMEM((3, 2, 64, 1280), BF16),
            pltpu.VMEM((3, 2, 64, 1280), BF16),
            pltpu.VMEM((3, 2, 64, 1280), F32),
            pltpu.VMEM((3, 64, 1280), BF16),
            pltpu.VMEM((3, 64, 1280), BF16),
            pltpu.SemaphoreType.DMA((COPIES,)),
            pltpu.SemaphoreType.DMA((COPIES,)),
            pltpu.SemaphoreType.DMA((11,)),
        ],
        compiler_params=pltpu.CompilerParams(
            collective_id=0, has_side_effects=True, vmem_limit_bytes=56 << 20
        ),
    )(pq, pk, pv, tq.reshape(64, 1024), tk.reshape(64, 128), tv.reshape(64, 128),
      tail_len, order.reshape(1, 128), weight)
    return pl.pallas_call(
        hand_over,
        out_shape=(jax.ShapeDtypeStruct((128, 1280), BF16), jax.ShapeDtypeStruct((1, 64, 1280), BF16)),
        in_specs=[vmem, vmem],
        out_specs=(vmem, vmem),
    )(prompt, tail.reshape(1, 64, 1280))


def solution(mesh):
    placed = (
        P("loop", "head"),
        P("loop", "head"),
        P("loop", "head"),
        P("loop", None, "head"),
        P("loop", None, "head"),
        P("loop", None, "head"),
        P("loop"),
        P(),
        P("head", None),
    )
    return jax.shard_map(
        on_device,
        mesh=mesh,
        in_specs=placed,
        out_specs=(P("loop", "head"), P("loop", None, "head")),
        check_vma=False,
    )
```
